256 devices in a mesh: dp: 2 (over x_lo), outer: 8 (over z), inner: 16 (over x_hi, y, core).
Axes of the slice: x: 4 (x_hi: 2, x_lo: 2; x = x_hi * 2 + x_lo), y: 4, z: 8, core: 2. Of those that a mesh axis runs over, the one named last changes fastest.
Arguments:
- queries: bfloat16 [65536, 1024], P(('dp', 'outer', 'inner')), parts along dimension 0, may hold values from -6 to 6
- keys: bfloat16 [65536, 128], P(('dp', 'outer', 'inner')), parts along dimension 0, may hold values from -6 to 6
- values: bfloat16 [65536, 128], P(('dp', 'outer', 'inner')), parts along dimension 0, may hold values from -6 to 6
- outputs: bfloat16 [65536, 1024], P(('dp', 'outer', 'inner')), parts along dimension 0, may hold values from -6 to 6
- out_grads: bfloat16 [65536, 1024], P(('dp', 'outer', 'inner')), parts along dimension 0, may hold values from -6 to 6
- log_sums: float32 [8, 65536], P(None, ('dp', 'outer', 'inner')), parts along dimension 1, may hold values from 6 to 9
- doc_lengths: int32 [64], P('dp'), parts along dimension 0, may hold values from 1 to 2048, 32768 in all
Outputs:
- query_grads: bfloat16 [65536, 1024], P(('dp', 'outer', 'inner')), parts along dimension 0
- key_grads: bfloat16 [65536, 128], P(('dp', 'outer', 'inner')), parts along dimension 0
- value_grads: bfloat16 [65536, 128], P(('dp', 'outer', 'inner')), parts along dimension 0
The draws below stay inside these ranges and needn't reach their ends.
There are 2 independent parts, one for each index of `dp`. The reference program is written for one: setup_inputs(seed, part) draws one part's arguments, and reference() takes and returns one part's arrays. A program takes and returns all parts, laid end to end along the dimension named above; each array names one. Nothing has to cross between parts.
Inputs may be any that keep to these rules, and one draw needn't show every extreme that they name: `doc_lengths`: each length is at least 1 and at most 2048, the lengths sum to 32768, and some document has exactly 2048 tokens.
All inputs are finite; a program needn't handle non-finite values.
Results may differ from the reference program's by a relative error of at most 0.01.
Values may be sent and summed in bfloat16 or wider, within the bound.
A program may use at most 64 MiB of HBM per device.

```python
import math
import jax
import jax.numpy as jnp
import numpy as np
from jax import lax

HEADS = 8
HEAD_DIM = 128
TOK_DEV = 256
TOKENS = 32768
MAX_DOC = 2048
NDOCS = 32


def levels(own_key, dims, split, low, top_value):
    factor_of = 1.0
    for position, shards_of in split:
        draws = jax.random.uniform(jax.random.fold_in(jax.random.fold_in(own_key, 6), position), (shards_of,), jnp.float32, low / len(split), top_value / len(split))
        factor_of = factor_of * jnp.repeat(jnp.exp(draws), dims[position] // shards_of).reshape((-1,) + (1,) * (len(dims) - 1 - position))
    return factor_of


def length_profile(number_of, total, most, lean):
    loads = [(1 << 20) // math.isqrt(rank ** lean) + 1 for rank in range(2, number_of + 1)]
    surplus, holding = total - most - (number_of - 1), [1] * (number_of - 1)
    while surplus > 0:
        free = [i for i in range(number_of - 1) if holding[i] < most]
        mass, budget = sum([loads[i] for i in free]), surplus
        for i in free:
            addition = min(most - holding[i], max(1, budget * loads[i] // mass), surplus)
            holding[i] = holding[i] + addition
            surplus = surplus - addition
    return np.array([most] + holding)


def ragged(key, amount, total, most, skew):
    if amount == 2:
        one = jax.random.randint(key, (), max(1, total - most), min(most, total - 1) + 1)
        return jnp.stack([one, total - one])
    tallies = jnp.asarray(length_profile(amount, total, most, skew), jnp.int32)
    pairs = (amount - 1) // 2
    source_of, taker = tallies[1:1 + 2 * pairs:2], tallies[2:2 + 2 * pairs:2]
    room = jnp.minimum(source_of - 1, most - taker)
    shifted = jax.random.randint(jax.random.fold_in(key, 1), (pairs,), 0, 1 << 20) % (room + 1)
    tallies = tallies.at[1:1 + 2 * pairs:2].set(source_of - shifted).at[2:2 + 2 * pairs:2].set(taker + shifted)
    return tallies[jax.random.permutation(jax.random.fold_in(key, 2), amount)]


def noise(rng, extent, deviation, limit, pieces=(), kind=jnp.bfloat16):
    entries = deviation * jax.random.normal(rng, extent, jnp.float32)
    if pieces:
        entries = entries * levels(rng, extent, pieces, -0.22, 0.18)
    return jnp.clip(entries, -limit, limit).astype(kind)


def setup_inputs(seed: int = 0, part: int = 0) -> dict:
    splits = jax.random.split(jax.random.key(seed), 8)
    part_keys = jax.random.split(jax.random.fold_in(splits[7], part), 8)
    return {
        "queries": noise(part_keys[0], (TOKENS, HEADS * HEAD_DIM), 1.0, 6.0, ((0, 128),)),
        "keys": noise(part_keys[1], (TOKENS, HEAD_DIM), 1.0, 6.0, ((0, 128),)),
        "values": noise(part_keys[2], (TOKENS, HEAD_DIM), 1.0, 6.0, ((0, 128),)),
        "outputs": noise(part_keys[3], (TOKENS, HEADS * HEAD_DIM), 1.0, 6.0, ((0, 128),)),
        "out_grads": noise(part_keys[4], (TOKENS, HEADS * HEAD_DIM), 1.0, 6.0, ((0, 128),)),
        "log_sums": jnp.clip(6.0 + 3.0 * jax.random.uniform(part_keys[5], (HEADS, TOKENS), jnp.float32) ** levels(part_keys[5], (HEADS, TOKENS), ((1, 128),), -0.2, 0.2), 6.0, 9.0),
        "doc_lengths": ragged(part_keys[6], NDOCS, TOKENS, MAX_DOC, 2).astype(jnp.int32),
    }


def doc_index(ends, positions):
    return jnp.sum((ends[None, :] <= positions[:, None]).astype(jnp.int32), axis=1)


def reference(queries, keys, values, outputs, out_grads, log_sums, doc_lengths):
    scale = 1.0 / (HEAD_DIM ** 0.5)
    ends = jnp.cumsum(doc_lengths).astype(jnp.int32)
    blocks = TOKENS // TOK_DEV
    window = MAX_DOC + TOK_DEV
    pad_keys = jnp.concatenate([jnp.zeros((MAX_DOC, HEAD_DIM), keys.dtype), keys], axis=0)
    pad_values = jnp.concatenate([jnp.zeros((MAX_DOC, HEAD_DIM), values.dtype), values], axis=0)
    rows = jnp.arange(TOK_DEV, dtype=jnp.int32)
    span_rows = jnp.arange(window, dtype=jnp.int32)

    def step(carry, block):
        acc_k, acc_v = carry
        start = (block * TOK_DEV).astype(jnp.int32)
        qblock = lax.dynamic_slice_in_dim(queries, start, TOK_DEV, 0).reshape(TOK_DEV, HEADS, HEAD_DIM)
        oblock = lax.dynamic_slice_in_dim(outputs, start, TOK_DEV, 0).reshape(TOK_DEV, HEADS, HEAD_DIM)
        gblock = lax.dynamic_slice_in_dim(out_grads, start, TOK_DEV, 0).reshape(TOK_DEV, HEADS, HEAD_DIM)
        lse = lax.dynamic_slice_in_dim(log_sums, start, TOK_DEV, 1)
        kwin = lax.dynamic_slice_in_dim(pad_keys, start, window, 0)
        vwin = lax.dynamic_slice_in_dim(pad_values, start, window, 0)
        qpos = start + rows
        kpos = start - MAX_DOC + span_rows
        qdoc = doc_index(ends, qpos)
        kdoc = doc_index(ends, kpos)
        allowed = (kpos[None, :] <= qpos[:, None]) & (kdoc[None, :] == qdoc[:, None]) & (kpos[None, :] >= 0)
        delta = jnp.sum(gblock.astype(jnp.float32) * oblock.astype(jnp.float32), axis=2)
        qf = qblock.astype(jnp.float32)
        gf = gblock.astype(jnp.float32)
        kf = kwin.astype(jnp.float32)
        vf = vwin.astype(jnp.float32)
        scores = jnp.einsum('qhd,kd->hqk', qf, kf) * scale
        prob = jnp.where(allowed[None], jnp.exp(scores - lse[:, :, None]), 0.0)
        prob_low = prob.astype(jnp.bfloat16).astype(jnp.float32)
        dv = jnp.einsum('hqk,qhd->kd', prob_low, gf)
        dprob = jnp.einsum('qhd,kd->hqk', gf, vf)
        dscore = (prob * (dprob - delta.T[:, :, None])).astype(jnp.bfloat16).astype(jnp.float32)
        dq = jnp.einsum('hqk,kd->qhd', dscore, kf) * scale
        dk = jnp.einsum('hqk,qhd->kd', dscore, qf) * scale
        acc_k = lax.dynamic_update_slice_in_dim(acc_k, lax.dynamic_slice_in_dim(acc_k, start, window, 0) + dk, start, 0)
        acc_v = lax.dynamic_update_slice_in_dim(acc_v, lax.dynamic_slice_in_dim(acc_v, start, window, 0) + dv, start, 0)
        return (acc_k, acc_v), dq.reshape(TOK_DEV, HEADS * HEAD_DIM).astype(jnp.bfloat16)

    zeros = jnp.zeros((MAX_DOC + TOKENS, HEAD_DIM), jnp.float32)
    (acc_k, acc_v), dqs = lax.scan(step, (zeros, zeros), jnp.arange(blocks, dtype=jnp.int32))
    query_grads = dqs.reshape(TOKENS, HEADS * HEAD_DIM)
    return query_grads, acc_k[MAX_DOC:].astype(jnp.bfloat16), acc_v[MAX_DOC:].astype(jnp.bfloat16)
```

```python
import functools
import math

import jax
import jax.numpy as jnp
from jax import lax
from jax.experimental import pallas as pl
from jax.experimental.pallas import tpu as pltpu
from jax.sharding import PartitionSpec as P

MESH = pl.DeviceIdType.MESH
F32 = jnp.float32
BF16 = jnp.bfloat16
HEADS = 8
DIM = 128
TOK = 256
REACH = 4


def nn(a, b):
    return lax.dot_general(a, b, (((1,), (0,)), ((), ())), preferred_element_type=F32)


def nt(a, b):
    return lax.dot_general(a, b, (((1,), (1,)), ((), ())), preferred_element_type=F32)


def kernel(
    outer, inner, q_hbm, k_hbm, v_hbm, o_hbm, g_hbm, lse_hbm, docs, dq_hbm, dk_out, dv_out,
    qs, gs, os, rows, kv, kt, bias, start, probs, ds, acc, own, ret_out, ret_in, dq_out, dq_in, dq_fin,
    load_sem, kv_send, kv_recv, ret_send, ret_recv, sib_send, sib_recv, store_sem,
):
    dp = lax.axis_index("dp")
    here = lax.axis_index("outer") * inner + lax.axis_index("inner")
    core = lax.rem(here, 2)
    total = outer * inner
    scale = 1.0 / DIM**0.5
    log2e = math.log2(math.e)

    def device(index):
        index = lax.rem(index + total, total)
        return (dp, index // inner, lax.rem(index, inner))

    sibling = device(here + 1 - 2 * core)

    loads = []

    def load(src, dst, n):
        copy = pltpu.make_async_copy(src, dst, load_sem.at[n])
        copy.start()
        loads.append(copy)

    load(k_hbm, kv.at[0, pl.ds(0, TOK)], 0)
    load(v_hbm, kv.at[0, pl.ds(TOK, TOK)], 1)
    for h in range(HEADS):
        load(q_hbm.at[:, pl.ds(h * DIM, DIM)], qs.at[0, pl.ds(h * TOK, TOK)], 2 + h)
        load(g_hbm.at[:, pl.ds(h * DIM, DIM)], gs.at[0, pl.ds(h * TOK, TOK)], 10 + h)
        load(o_hbm.at[:, pl.ds(h * DIM, DIM)], os.at[pl.ds(h * TOK, TOK)], 18 + h)
    load(lse_hbm, rows.at[0, pl.ds(0, HEADS)], 26)

    barrier = pltpu.get_barrier_semaphore()
    pl.semaphore_signal(barrier, inc=1, device_id=sibling, device_id_type=MESH)
    for k in range(1, REACH + 1):
        for way in (1, -1):
            pl.semaphore_signal(barrier, inc=1, device_id=device(here + way * 2 * k), device_id_type=MESH)

    lane = lax.broadcasted_iota(jnp.int32, (8, TOK), 1)
    first = here * TOK
    other = (here + 1 - 2 * core) * TOK
    end = jnp.int32(0)
    low = [jnp.zeros((8, TOK), jnp.int32) for _ in range(2)]
    for d in range(docs.shape[0]):
        end = end + docs[d]
        low = [
            jnp.where(lane + base >= end, end, x) for base, x in zip((first, other), low)
        ]
    start[0] = low[0]
    start[1] = low[1]

    pl.semaphore_wait(barrier, 2 * REACH + 1)
    for copy in loads[:2]:
        copy.wait()

    def kv_copy(k):
        return pltpu.make_async_remote_copy(
            src_ref=kv.at[0], dst_ref=kv.at[k], send_sem=kv_send.at[k], recv_sem=kv_recv.at[k],
            device_id=device(here + 2 * k), device_id_type=MESH,
        )

    def ret_copy(k):
        return pltpu.make_async_remote_copy(
            src_ref=ret_out.at[k], dst_ref=ret_in.at[k], send_sem=ret_send.at[k], recv_sem=ret_recv.at[k],
            device_id=device(here - 2 * k), device_id_type=MESH,
        )

    def sib_copy(src, dst, n):
        return pltpu.make_async_remote_copy(
            src_ref=src, dst_ref=dst, send_sem=sib_send.at[n], recv_sem=sib_recv.at[n],
            device_id=sibling, device_id_type=MESH,
        )

    for k in range(1, REACH + 1):
        kv_copy(k).start()
    for copy in loads[2:]:
        copy.wait()
    to_sib = [sib_copy(qs.at[0], qs.at[1], 0), sib_copy(gs.at[0], gs.at[1], 1)]
    for copy in to_sib:
        copy.start()

    row = lax.broadcasted_iota(jnp.int32, (HEADS, DIM), 0)
    delta = jnp.zeros((HEADS, TOK), F32)
    for h in range(HEADS):
        part = pl.ds(h * TOK, TOK)
        prod = gs[0, part, :].astype(F32) * os[part, :].astype(F32)
        hi = prod.astype(BF16)
        lo = (prod - hi.astype(F32)).astype(BF16)
        pick = jnp.where(row == h, 1.0, 0.0).astype(BF16)
        delta = delta + (nt(pick, hi) + nt(pick, lo))
    rows[0, HEADS:, :] = delta
    rows[0, :HEADS, :] = rows[0, :HEADS, :] * log2e
    to_sib.append(sib_copy(rows.at[0], rows.at[1], 2))
    to_sib[2].start()

    def pair(k, a):
        query_base = lax.select(a == 0, first, other)
        key_base = (here - 2 * k) * TOK
        t = key_base + lax.broadcasted_iota(jnp.int32, (TOK, TOK), 0)
        p = query_base + lax.broadcasted_iota(jnp.int32, (TOK, TOK), 1)
        ok = (t >= start[a, 0:1, :]) & (t <= p)
        bias[...] = jnp.where(ok, 0.0, -jnp.inf)
        keys = kv[k, :TOK, :]
        values = kv[k, TOK:, :]
        for h in range(HEADS):
            part = pl.ds(h * TOK, TOK)
            scores = nt(keys, qs[a, part, :])
            dprob = nt(values, gs[a, part, :])
            prob = jnp.exp2(scores * (scale * log2e) - rows[a, h : h + 1, :] + bias[...])
            dscore = prob * (dprob - rows[a, HEADS + h : HEADS + h + 1, :])
            probs[:, h * TOK : (h + 1) * TOK] = prob.astype(BF16)
            ds[a, k, :, h * TOK : (h + 1) * TOK] = dscore.astype(BF16)
        acc[:TOK, :] += nn(ds[a, k], qs[a])
        acc[TOK:, :] += nn(probs[...], gs[a])

    def block(k, _):
        @pl.when(k > 0)
        def _():
            kv_copy(k).wait_recv()

        kt[k] = kv[k, :TOK, :].T
        acc[...] = jnp.zeros_like(acc)
        pair(k, 0)

        @pl.when(k == core)
        def _():
            for copy in to_sib:
                copy.wait_recv()

        @pl.when((k >= core) & (k < core + REACH))
        def _():
            pair(k, 1)

        acc[:TOK, :] = acc[:TOK, :] * scale

        @pl.when(k == 0)
        def _():
            own[...] = acc[...]

        @pl.when(k > 0)
        def _():
            ret_out[k] = acc[...].astype(BF16)
            ret_copy(k).start()

        return 0

    lax.fori_loop(0, REACH + 1, block, 0)

    for h in range(HEADS):
        cols = pl.ds(h * TOK, TOK)
        part = sum(nn(kt[core + m], ds[1, core + m, :, cols]) for m in range(REACH))
        dq_out[h] = (part * scale).astype(BF16)
    dq_copy = sib_copy(dq_out, dq_in, 3)
    dq_copy.start()
    for copy in to_sib:
        copy.wait_send()
    dq_copy.wait_recv()
    for h in range(HEADS):
        cols = pl.ds(h * TOK, TOK)
        part = sum(nn(kt[m], ds[0, m, :, cols]) for m in range(REACH + 1))
        both = part * scale + dq_in[h].astype(F32)
        dq_fin[:, h * DIM : (h + 1) * DIM] = both.T.astype(BF16)
    store = pltpu.make_async_copy(dq_fin, dq_hbm, store_sem)
    store.start()

    grads = own[...]
    for k in range(1, REACH + 1):
        ret_copy(k).wait_recv()
        grads = grads + ret_in[k].astype(F32)
    dk_out[...] = grads[:TOK].astype(BF16)
    dv_out[...] = grads[TOK:].astype(BF16)

    dq_copy.wait_send()
    for k in range(1, REACH + 1):
        kv_copy(k).wait_send()
        ret_copy(k).wait_send()
    store.wait()


def local(outer, inner, queries, keys, values, outputs, out_grads, log_sums, doc_lengths):
    wide = HEADS * TOK
    anywhere = pl.BlockSpec(memory_space=pl.ANY)
    vmem = pl.BlockSpec(memory_space=pltpu.VMEM)
    dma = pltpu.SemaphoreType.DMA
    return pl.pallas_call(
        functools.partial(kernel, outer, inner),
        out_shape=[
            jax.ShapeDtypeStruct((TOK, HEADS * DIM), BF16),
            jax.ShapeDtypeStruct((TOK, DIM), BF16),
            jax.ShapeDtypeStruct((TOK, DIM), BF16),
        ],
        in_specs=[anywhere] * 6 + [pl.BlockSpec(memory_space=pltpu.SMEM)],
        out_specs=[anywhere, vmem, vmem],
        scratch_shapes=[
            pltpu.VMEM((2, wide, DIM), BF16),
            pltpu.VMEM((2, wide, DIM), BF16),
            pltpu.VMEM((wide, DIM), BF16),
            pltpu.VMEM((2, 2 * HEADS, TOK), F32),
            pltpu.VMEM((REACH + 1, 2 * TOK, DIM), BF16),
            pltpu.VMEM((REACH + 1, DIM, TOK), BF16),
            pltpu.VMEM((TOK, TOK), F32),
            pltpu.VMEM((2, 8, TOK), jnp.int32),
            pltpu.VMEM((TOK, wide), BF16),
            pltpu.VMEM((2, REACH + 1, TOK, wide), BF16),
            pltpu.VMEM((2 * TOK, DIM), F32),
            pltpu.VMEM((2 * TOK, DIM), F32),
            pltpu.VMEM((REACH + 1, 2 * TOK, DIM), BF16),
            pltpu.VMEM((REACH + 1, 2 * TOK, DIM), BF16),
            pltpu.VMEM((HEADS, DIM, TOK), BF16),
            pltpu.VMEM((HEADS, DIM, TOK), BF16),
            pltpu.VMEM((TOK, HEADS * DIM), BF16),
            dma((27,)),
            dma((REACH + 1,)),
            dma((REACH + 1,)),
            dma((REACH + 1,)),
            dma((REACH + 1,)),
            dma((4,)),
            dma((4,)),
            dma,
        ],
        compiler_params=pltpu.CompilerParams(
            collective_id=0, has_side_effects=True, vmem_limit_bytes=48 << 20
        ),
        name="attention_backward",
    )(queries, keys, values, outputs, out_grads, log_sums, doc_lengths)


def solution(mesh):
    rows = P(("dp", "outer", "inner"), None)
    return jax.shard_map(
        functools.partial(local, mesh.shape["outer"], mesh.shape["inner"]),
        mesh=mesh,
        in_specs=(rows,) * 5 + (P(None, ("dp", "outer", "inner")), P("dp")),
        out_specs=(rows,) * 3,
        check_vma=False,
    )
```

```python
import functools
import math

import jax
import jax.numpy as jnp
from jax import lax
from jax.experimental import pallas as pl
from jax.experimental.pallas import tpu as pltpu
from jax.sharding import PartitionSpec as P

MESH = pl.DeviceIdType.MESH
F32 = jnp.float32
BF16 = jnp.bfloat16
HEADS = 8
DIM = 128
TOK = 256
REACH = 4


def nn(a, b):
    return lax.dot_general(a, b, (((1,), (0,)), ((), ())), preferred_element_type=F32)


def nt(a, b):
    return lax.dot_general(a, b, (((1,), (1,)), ((), ())), preferred_element_type=F32)


def kernel(
    outer, inner, q_hbm, k_hbm, v_hbm, o_hbm, g_hbm, lse_hbm, docs, dq_hbm, dk_hbm, dv_hbm,
    qs, gs, os, rows, kv, kt, bias, start, probs, ds, acc, own, ret_out, ret_in, dq_out, dq_in, dq_fin, dkv_fin,
    load_sem, kv_send, kv_recv, ret_send, ret_recv, sib_send, sib_recv, store_sem,
):
    dp = lax.axis_index("dp")
    here = lax.axis_index("outer") * inner + lax.axis_index("inner")
    core = lax.rem(here, 2)
    total = outer * inner
    scale = 1.0 / DIM**0.5
    log2e = math.log2(math.e)

    def device(index):
        index = lax.rem(index + total, total)
        return (dp, index // inner, lax.rem(index, inner))

    sibling = device(here + 1 - 2 * core)

    def ahead(k):
        return here + 2 * k < total

    def behind(k):
        return here - 2 * k >= 0

    barrier = pltpu.get_barrier_semaphore()
    pl.semaphore_signal(barrier, inc=1, device_id=sibling, device_id_type=MESH)
    for k in range(1, REACH + 1):
        for reaches, way in ((ahead, 1), (behind, -1)):

            @pl.when(reaches(k))
            def _():
                pl.semaphore_signal(
                    barrier, inc=1, device_id=device(here + way * 2 * k), device_id_type=MESH
                )

    loads = []

    def load(src, dst, n):
        copy = pltpu.make_async_copy(src, dst, load_sem.at[n])
        copy.start()
        loads.append(copy)

    load(k_hbm, kv.at[0, pl.ds(0, TOK)], 0)
    load(v_hbm, kv.at[0, pl.ds(TOK, TOK)], 1)
    for h in range(HEADS):
        load(q_hbm.at[:, pl.ds(h * DIM, DIM)], qs.at[0, pl.ds(h * TOK, TOK)], 2 + h)
        load(g_hbm.at[:, pl.ds(h * DIM, DIM)], gs.at[0, pl.ds(h * TOK, TOK)], 10 + h)
        load(o_hbm.at[:, pl.ds(h * DIM, DIM)], os.at[pl.ds(h * TOK, TOK)], 18 + h)
    load(lse_hbm, rows.at[0, pl.ds(0, HEADS)], 26)

    greeted = jnp.int32(1)
    for k in range(1, REACH + 1):
        for reaches in (ahead, behind):
            greeted = greeted + jnp.where(reaches(k), 1, 0)
    pl.semaphore_wait(barrier, greeted)
    for copy in loads[:2]:
        copy.wait()

    def kv_copy(k):
        return pltpu.make_async_remote_copy(
            src_ref=kv.at[0], dst_ref=kv.at[k], send_sem=kv_send.at[k], recv_sem=kv_recv.at[k],
            device_id=device(here + 2 * k), device_id_type=MESH,
        )

    def ret_copy(k):
        return pltpu.make_async_remote_copy(
            src_ref=ret_out.at[k], dst_ref=ret_in.at[k], send_sem=ret_send.at[k], recv_sem=ret_recv.at[k],
            device_id=device(here - 2 * k), device_id_type=MESH,
        )

    def sib_copy(src, dst, n):
        return pltpu.make_async_remote_copy(
            src_ref=src, dst_ref=dst, send_sem=sib_send.at[n], recv_sem=sib_recv.at[n],
            device_id=sibling, device_id_type=MESH,
        )

    for k in range(1, REACH + 1):
        pl.when(ahead(k))(kv_copy(k).start)

    for copy in loads[2:]:
        copy.wait()
    to_sib = [sib_copy(qs.at[0], qs.at[1], 0), sib_copy(gs.at[0], gs.at[1], 1)]
    for copy in to_sib:
        copy.start()

    lane = lax.broadcasted_iota(jnp.int32, (8, TOK), 1)
    first = here * TOK
    other = (here + 1 - 2 * core) * TOK
    end = jnp.int32(0)
    low = [jnp.zeros((8, TOK), jnp.int32) for _ in range(2)]
    for d in range(docs.shape[0]):
        end = end + docs[d]
        low = [
            jnp.where(lane + base >= end, end, x) for base, x in zip((first, other), low)
        ]
    start[0] = low[0]
    start[1] = low[1]

    row = lax.broadcasted_iota(jnp.int32, (HEADS, DIM), 0)
    delta = jnp.zeros((HEADS, TOK), F32)
    for h in range(HEADS):
        part = pl.ds(h * TOK, TOK)
        prod = gs[0, part, :].astype(F32) * os[part, :].astype(F32)
        hi = prod.astype(BF16)
        lo = (prod - hi.astype(F32)).astype(BF16)
        pick = jnp.where(row == h, 1.0, 0.0).astype(BF16)
        delta = delta + (nt(pick, hi) + nt(pick, lo))
    rows[0, HEADS:, :] = delta
    rows[0, :HEADS, :] = rows[0, :HEADS, :] * log2e
    to_sib.append(sib_copy(rows.at[0], rows.at[1], 2))
    to_sib[2].start()

    def pair(k, a):
        query_base = lax.select(a == 0, first, other)
        key_base = (here - 2 * k) * TOK
        t = key_base + lax.broadcasted_iota(jnp.int32, (TOK, TOK), 0)
        p = query_base + lax.broadcasted_iota(jnp.int32, (TOK, TOK), 1)
        ok = (t >= start[a, 0:1, :]) & (t <= p)
        bias[...] = jnp.where(ok, 0.0, -jnp.inf)
        keys = kv[k, :TOK, :]
        values = kv[k, TOK:, :]
        for h in range(HEADS):
            part = pl.ds(h * TOK, TOK)
            scores = nt(keys, qs[a, part, :])
            dprob = nt(values, gs[a, part, :])
            prob = jnp.exp2(scores * (scale * log2e) - rows[a, h : h + 1, :] + bias[...])
            dscore = prob * (dprob - rows[a, HEADS + h : HEADS + h + 1, :])
            probs[:, h * TOK : (h + 1) * TOK] = prob.astype(BF16)
            ds[a, k, :, h * TOK : (h + 1) * TOK] = dscore.astype(BF16)
        acc[:TOK, :] += nn(ds[a, k], qs[a])
        acc[TOK:, :] += nn(probs[...], gs[a])

    y = lax.rem(here // 2, REACH)
    orders = ((4, 3, 1, 2), (1, 4, 3, 2), (1, 4, 2, 3), (1, 3, 2, 4))

    def block(step, _):
        k = jnp.int32(0)
        for place, order in enumerate(orders):
            for n, back in enumerate(order):
                k = jnp.where((y == place) & (step == n + 1), back, k)

        @pl.when((k > 0) & behind(k))
        def _():
            kv_copy(k).wait_recv()

        @pl.when((k > 0) & ~behind(k))
        def _():
            kv[k] = jnp.zeros_like(kv[k])

        kt[k] = kv[k, :TOK, :].T
        acc[...] = jnp.zeros_like(acc)
        pair(k, 0)

        @pl.when(step == core)
        def _():
            for copy in to_sib:
                copy.wait_recv()

        @pl.when((k >= core) & (k < core + REACH))
        def _():
            pair(k, 1)

        acc[:TOK, :] = acc[:TOK, :] * scale

        @pl.when(k == 0)
        def _():
            own[...] = acc[...]

        @pl.when((k > 0) & behind(k))
        def _():
            ret_out[k] = acc[...].astype(BF16)
            ret_copy(k).start()

        return 0

    lax.fori_loop(0, REACH + 1, block, 0)

    for h in range(HEADS):
        cols = pl.ds(h * TOK, TOK)
        part = sum(nn(kt[core + m], ds[1, core + m, :, cols]) for m in range(REACH))
        dq_out[h] = (part * scale).astype(BF16)
    dq_copy = sib_copy(dq_out, dq_in, 3)
    dq_copy.start()
    for copy in to_sib:
        copy.wait_send()
    dq_copy.wait_recv()
    for h in range(HEADS):
        cols = pl.ds(h * TOK, TOK)
        part = sum(nn(kt[m], ds[0, m, :, cols]) for m in range(REACH + 1))
        both = part * scale + dq_in[h].astype(F32)
        dq_fin[:, h * DIM : (h + 1) * DIM] = both.T.astype(BF16)
    store = pltpu.make_async_copy(dq_fin, dq_hbm, store_sem.at[0])
    store.start()

    for k in range(1, REACH + 1):

        @pl.when(ahead(k))
        def _():
            ret_copy(k).wait_recv()
            own[...] += ret_in[k].astype(F32)

    dkv_fin[...] = own[...].astype(BF16)
    stores = [store]
    for n, ref in enumerate((dk_hbm, dv_hbm)):
        stores.append(pltpu.make_async_copy(dkv_fin.at[pl.ds(n * TOK, TOK)], ref, store_sem.at[n + 1]))
        stores[-1].start()

    dq_copy.wait_send()
    for k in range(1, REACH + 1):
        pl.when(ahead(k))(kv_copy(k).wait_send)
        pl.when(behind(k))(ret_copy(k).wait_send)
    for copy in stores:
        copy.wait()


def finish(dq_in, dk_in, dv_in, dq_out, dk_out, dv_out, dq, dk, dv, in_sem, out_sem):
    parts = 4
    rows = TOK // parts
    moves = [
        (dq_in.at[pl.ds(n * rows, rows)], dq.at[pl.ds(n * rows, rows)], dq_out.at[pl.ds(n * rows, rows)])
        for n in range(parts)
    ]
    moves += [(dk_in, dk, dk_out), (dv_in, dv, dv_out)]
    reads = [pltpu.make_async_copy(a, b, in_sem.at[n]) for n, (a, b, _) in enumerate(moves)]
    writes = [pltpu.make_async_copy(b, c, out_sem.at[n]) for n, (_, b, c) in enumerate(moves)]
    for read in reads:
        read.start()
    for read, write in zip(reads, writes):
        read.wait()
        write.start()
    for write in writes:
        write.wait()


def local(outer, inner, queries, keys, values, outputs, out_grads, log_sums, doc_lengths):
    wide = HEADS * TOK
    anywhere = pl.BlockSpec(memory_space=pl.ANY)
    dma = pltpu.SemaphoreType.DMA
    grads = pl.pallas_call(
        functools.partial(kernel, outer, inner),
        out_shape=[
            jax.ShapeDtypeStruct((TOK, HEADS * DIM), BF16),
            jax.ShapeDtypeStruct((TOK, DIM), BF16),
            jax.ShapeDtypeStruct((TOK, DIM), BF16),
        ],
        in_specs=[anywhere] * 6 + [pl.BlockSpec(memory_space=pltpu.SMEM)],
        out_specs=[anywhere] * 3,
        scratch_shapes=[
            pltpu.VMEM((2, wide, DIM), BF16),
            pltpu.VMEM((2, wide, DIM), BF16),
            pltpu.VMEM((wide, DIM), BF16),
            pltpu.VMEM((2, 2 * HEADS, TOK), F32),
            pltpu.VMEM((REACH + 1, 2 * TOK, DIM), BF16),
            pltpu.VMEM((REACH + 1, DIM, TOK), BF16),
            pltpu.VMEM((TOK, TOK), F32),
            pltpu.VMEM((2, 8, TOK), jnp.int32),
            pltpu.VMEM((TOK, wide), BF16),
            pltpu.VMEM((2, REACH + 1, TOK, wide), BF16),
            pltpu.VMEM((2 * TOK, DIM), F32),
            pltpu.VMEM((2 * TOK, DIM), F32),
            pltpu.VMEM((REACH + 1, 2 * TOK, DIM), BF16),
            pltpu.VMEM((REACH + 1, 2 * TOK, DIM), BF16),
            pltpu.VMEM((HEADS, DIM, TOK), BF16),
            pltpu.VMEM((HEADS, DIM, TOK), BF16),
            pltpu.VMEM((TOK, HEADS * DIM), BF16),
            pltpu.VMEM((2 * TOK, DIM), BF16),
            dma((27,)),
            dma((REACH + 1,)),
            dma((REACH + 1,)),
            dma((REACH + 1,)),
            dma((REACH + 1,)),
            dma((4,)),
            dma((4,)),
            dma((3,)),
        ],
        compiler_params=pltpu.CompilerParams(
            collective_id=0, has_side_effects=True, vmem_limit_bytes=60 << 20
        ),
        name="attention_backward",
    )(queries, keys, values, outputs, out_grads, log_sums, doc_lengths)
    shapes = [(TOK, HEADS * DIM), (TOK, DIM), (TOK, DIM)]
    return pl.pallas_call(
        finish,
        out_shape=[jax.ShapeDtypeStruct(shape, BF16) for shape in shapes],
        in_specs=[anywhere] * 3,
        out_specs=[anywhere] * 3,
        scratch_shapes=[pltpu.VMEM(shape, BF16) for shape in shapes] + [dma((6,)), dma((6,))],
        compiler_params=pltpu.CompilerParams(vmem_limit_bytes=60 << 20),
        name="finish",
    )(*grads)


def solution(mesh):
    rows = P(("dp", "outer", "inner"), None)
    return jax.shard_map(
        functools.partial(local, mesh.shape["outer"], mesh.shape["inner"]),
        mesh=mesh,
        in_specs=(rows,) * 5 + (P(None, ("dp", "outer", "inner")), P("dp")),
        out_specs=(rows,) * 3,
        check_vma=False,
    )
```

```python
import functools
import math

import jax
import jax.numpy as jnp
from jax import lax
from jax.experimental import pallas as pl
from jax.experimental.pallas import tpu as pltpu
from jax.sharding import PartitionSpec as P

MESH = pl.DeviceIdType.MESH
F32 = jnp.float32
BF16 = jnp.bfloat16
HEADS = 8
DIM = 128
TOK = 256
GROUP = 2
REACH = 4


def nn(a, b):
    return lax.dot_general(a, b, (((1,), (0,)), ((), ())), preferred_element_type=F32)


def nt(a, b):
    return lax.dot_general(a, b, (((1,), (1,)), ((), ())), preferred_element_type=F32)


def kernel(
    outer, inner, q_hbm, k_hbm, v_hbm, o_hbm, g_hbm, lse_hbm, docs_hbm, dq_fin, own, ret_in,
    docs, qs, gs, qt, gt, os, rows, cols, kv, bias, start, probs, ds, acc, ret_out, dq_out, dq_in,
    load_sem, kv_send, kv_recv, ret_send, ret_recv, sib_send, sib_recv,
):
    dp = lax.axis_index("dp")
    here = lax.axis_index("outer") * inner + lax.axis_index("inner")
    core = lax.rem(here, 2)
    y = lax.rem(here // 2, REACH)
    total = outer * inner
    scale = 1.0 / DIM**0.5
    log2e = math.log2(math.e)

    def device(index):
        index = lax.rem(index + total, total)
        return (dp, index // inner, lax.rem(index, inner))

    sibling = device(here + 1 - 2 * core)

    def ahead(k):
        return here + 2 * k < total

    def behind(k):
        return here - 2 * k >= 0

    barrier = pltpu.get_barrier_semaphore()
    pl.semaphore_signal(barrier, inc=1, device_id=sibling, device_id_type=MESH)
    for k in range(1, REACH + 1):
        for reaches, way in ((ahead, 1), (behind, -1)):

            @pl.when(reaches(k))
            def _():
                pl.semaphore_signal(
                    barrier, inc=1, device_id=device(here + way * 2 * k), device_id_type=MESH
                )

    loads = []

    def load(src, dst, n):
        copy = pltpu.make_async_copy(src, dst, load_sem.at[n])
        copy.start()
        loads.append(copy)

    load(k_hbm, kv.at[0, pl.ds(0, TOK)], 0)
    load(v_hbm, kv.at[0, pl.ds(TOK, TOK)], 1)
    for h in range(HEADS):
        load(q_hbm.at[:, pl.ds(h * DIM, DIM)], qs.at[0, pl.ds(h * TOK, TOK)], 2 + h)
        load(g_hbm.at[:, pl.ds(h * DIM, DIM)], gs.at[0, pl.ds(h * TOK, TOK)], 10 + h)
        load(o_hbm.at[:, pl.ds(h * DIM, DIM)], os.at[pl.ds(h * TOK, TOK)], 18 + h)
    load(lse_hbm, rows.at[0, pl.ds(0, HEADS)], 26)
    load(docs_hbm, docs, 27)

    greeted = jnp.int32(1)
    for k in range(1, REACH + 1):
        for reaches in (ahead, behind):
            greeted = greeted + jnp.where(reaches(k), 1, 0)
    pl.semaphore_wait(barrier, greeted)
    for copy in loads[:2]:
        copy.wait()

    def kv_copy(k):
        return pltpu.make_async_remote_copy(
            src_ref=kv.at[0], dst_ref=kv.at[k], send_sem=kv_send.at[k], recv_sem=kv_recv.at[k],
            device_id=device(here + 2 * k), device_id_type=MESH,
        )

    def ret_copy(k):
        return pltpu.make_async_remote_copy(
            src_ref=ret_out.at[k], dst_ref=ret_in.at[k], send_sem=ret_send.at[k], recv_sem=ret_recv.at[k],
            device_id=device(here - 2 * k), device_id_type=MESH,
        )

    def sib_copy(src, dst, n):
        return pltpu.make_async_remote_copy(
            src_ref=src, dst_ref=dst, send_sem=sib_send.at[n], recv_sem=sib_recv.at[n],
            device_id=sibling, device_id_type=MESH,
        )

    def send(slot):
        def start(k):
            kv_copy(k).start()

        pl.when((slot <= y) & ahead(REACH - y + slot))(lambda: start(REACH - y + slot))
        pl.when(slot + y <= REACH - 2)(lambda: start(slot + 1))

    for z_ in range(4):
        send(z_)
    for copy in loads[2:]:
        copy.wait()
    to_sib = [sib_copy(qs.at[0], qs.at[1], 0), sib_copy(gs.at[0], gs.at[1], 1)]
    for copy in to_sib:
        copy.start()

    line = lax.broadcasted_iota(jnp.int32, (TOK, DIM), 0)
    first = here * TOK
    other = (here + 1 - 2 * core) * TOK
    end = jnp.int32(0)
    low = [jnp.zeros((TOK, DIM), jnp.int32) for _ in range(2)]
    for d in range(docs.shape[0]):
        end = end + docs[d]
        low = [jnp.where(line + base >= end, end, x) for base, x in zip((first, other), low)]
    start[0] = low[0]
    start[1] = low[1]

    row = lax.broadcasted_iota(jnp.int32, (HEADS, DIM), 0)
    delta = jnp.zeros((HEADS, TOK), F32)
    for h in range(HEADS):
        part = pl.ds(h * TOK, TOK)
        prod = gs[0, part, :].astype(F32) * os[part, :].astype(F32)
        hi = prod.astype(BF16)
        lo = (prod - hi.astype(F32)).astype(BF16)
        pick = jnp.where(row == h, 1.0, 0.0).astype(BF16)
        delta = delta + (nt(pick, hi) + nt(pick, lo))
    rows[0, HEADS:, :] = delta
    rows[0, :HEADS, :] = rows[0, :HEADS, :] * log2e
    to_sib.append(sib_copy(rows.at[0], rows.at[1], 2))
    to_sib[2].start()

    def prepare(a):
        left = rows[a]
        terms = []
        for _ in range(3):
            terms.append(left.astype(BF16))
            left = left - terms[-1].astype(F32)
        columns = jnp.concatenate(terms, axis=0).T
        place = lax.broadcasted_iota(jnp.int32, (6 * HEADS, DIM), 0)
        for n in range(2 * HEADS):
            pick = jnp.where(lax.rem(place, 2 * HEADS) == n, 1.0, 0.0).astype(BF16)
            cols[a, n] = nn(columns, pick)
        for h in range(HEADS):
            part = pl.ds(h * TOK, TOK)
            qt[a, :, part] = qs[a, part, :].T
            gt[a, :, part] = gs[a, part, :].T

    def twice(x):
        return jnp.concatenate([x, x], axis=1)

    def pair(k, a):
        query_base = lax.select(a == 0, first, other)
        key_base = (here - 2 * k) * TOK
        p = query_base + lax.broadcasted_iota(jnp.int32, (TOK, TOK), 0)
        t = key_base + lax.broadcasted_iota(jnp.int32, (TOK, TOK), 1)
        ok = (t >= twice(start[a])) & (t <= p)
        bias[...] = jnp.where(ok, 0.0, -jnp.inf)
        keys = kv[k, :TOK, :]
        values = kv[k, TOK:, :]
        for n in range(HEADS // GROUP):
            part = pl.ds(n * GROUP * TOK, GROUP * TOK)
            scores = nt(qs[a, part, :], keys)
            dprob = nt(gs[a, part, :], values)
            for m in range(GROUP):
                h = n * GROUP + m
                mine = slice(m * TOK, (m + 1) * TOK)
                out = pl.ds(h * TOK, TOK)
                prob = jnp.exp2(scores[mine] * (scale * log2e) - twice(cols[a, h]) + bias[...])
                dscore = prob * (dprob[mine] - twice(cols[a, HEADS + h]))
                probs[out, :] = prob.astype(BF16)
                ds[a, k, out, :] = dscore.astype(BF16)
        acc[:DIM, :] += nn(qt[a], ds[a, k])
        acc[DIM:, :] += nn(gt[a], probs[...])

    orders = ((4, 3, 1, 2), (1, 4, 3, 2), (1, 4, 2, 3), (1, 3, 2, 4))

    prepare(0)

    def item(n, _):
        step, a = n // 2, lax.rem(n, 2)
        k = jnp.int32(0)
        for place, order in enumerate(orders):
            for m, back in enumerate(order):
                k = jnp.where((y == place) & (step == m + 1), back, k)

        @pl.when(n == 1)
        def _():
            for copy in to_sib:
                copy.wait_recv()
            prepare(1)


        @pl.when((a == 0) & (k > 0) & behind(k))
        def _():
            kv_copy(k).wait_recv()


        @pl.when((a == 0) & (k > 0) & ~behind(k))
        def _():
            kv[k] = jnp.zeros_like(kv[k])

        @pl.when(a == 0)
        def _():
            acc[...] = jnp.zeros_like(acc)

        @pl.when((a == 0) | ((k >= core) & (k < core + REACH)))
        def _():
            pair(k, a)

        @pl.when((a == 1) & (k == 0))
        def _():
            own[:DIM, :] = acc[:DIM, :] * scale
            own[DIM:, :] = acc[DIM:, :]

        @pl.when((a == 1) & (k > 0) & behind(k))
        def _():
            ret_out[k, :DIM, :] = (acc[:DIM, :] * scale).astype(BF16)
            ret_out[k, DIM:, :] = acc[DIM:, :].astype(BF16)
            ret_copy(k).start()

        return 0

    lax.fori_loop(0, 2 * (REACH + 1), item, 0)

    part = sum(nn(ds[1, core + m], kv[core + m, :TOK, :]) for m in range(REACH))
    dq_out[...] = (part * scale).astype(BF16)
    dq_copy = sib_copy(dq_out, dq_in, 3)
    dq_copy.start()
    for copy in to_sib:
        copy.wait_send()
    part = sum(nn(ds[0, m], kv[m, :TOK, :]) for m in range(REACH + 1)) * scale
    dq_copy.wait_recv()
    both = part + dq_in[...].astype(F32)
    for h in range(HEADS):
        dq_fin[:, h * DIM : (h + 1) * DIM] = both[h * TOK : (h + 1) * TOK].astype(BF16)
    dq_copy.wait_send()
    for k in range(1, REACH + 1):
        pl.when(ahead(k))(kv_copy(k).wait_send)
        pl.when(behind(k))(ret_copy(k).wait_send)
    for k in range(1, REACH + 1):
        pl.when(ahead(k))(ret_copy(k).wait_recv)


def finish(outer, inner, dq, own, ret, dq_out, dk_out, dv_out, dk, dv, sem):
    here = lax.axis_index("outer") * inner + lax.axis_index("inner")
    writes = [
        pltpu.make_async_copy(a, b, sem.at[n])
        for n, (a, b) in enumerate(((dq, dq_out), (dk, dk_out), (dv, dv_out)))
    ]
    writes[0].start()
    total = own[...]
    for k in range(1, REACH + 1):
        total = total + jnp.where(here + 2 * k < outer * inner, ret[k].astype(F32), 0.0)
    dk[...] = total[:DIM, :].T.astype(BF16)
    writes[1].start()
    dv[...] = total[DIM:, :].T.astype(BF16)
    writes[2].start()
    for write in writes:
        write.wait()


def local(outer, inner, queries, keys, values, outputs, out_grads, log_sums, doc_lengths):
    wide = HEADS * TOK
    anywhere = pl.BlockSpec(memory_space=pl.ANY)
    dma = pltpu.SemaphoreType.DMA
    grads = pl.pallas_call(
        functools.partial(kernel, outer, inner),
        out_shape=[
            jax.ShapeDtypeStruct((TOK, HEADS * DIM), BF16),
            jax.ShapeDtypeStruct((2 * DIM, TOK), F32),
            jax.ShapeDtypeStruct((REACH + 1, 2 * DIM, TOK), BF16),
        ],
        in_specs=[anywhere] * 7,
        out_specs=[pl.BlockSpec(memory_space=pltpu.VMEM)] * 3,
        scratch_shapes=[
            pltpu.SMEM(doc_lengths.shape, jnp.int32),
            pltpu.VMEM((2, wide, DIM), BF16),
            pltpu.VMEM((2, wide, DIM), BF16),
            pltpu.VMEM((2, DIM, wide), BF16),
            pltpu.VMEM((2, DIM, wide), BF16),
            pltpu.VMEM((wide, DIM), BF16),
            pltpu.VMEM((2, 2 * HEADS, TOK), F32),
            pltpu.VMEM((2, 2 * HEADS, TOK, DIM), F32),
            pltpu.VMEM((REACH + 1, 2 * TOK, DIM), BF16),
            pltpu.VMEM((TOK, TOK), F32),
            pltpu.VMEM((2, TOK, DIM), jnp.int32),
            pltpu.VMEM((wide, TOK), BF16),
            pltpu.VMEM((2, REACH + 1, wide, TOK), BF16),
            pltpu.VMEM((2 * DIM, TOK), F32),
            pltpu.VMEM((REACH + 1, 2 * DIM, TOK), BF16),
            pltpu.VMEM((wide, DIM), BF16),
            pltpu.VMEM((wide, DIM), BF16),
            dma((28,)),
            dma((REACH + 1,)),
            dma((REACH + 1,)),
            dma((REACH + 1,)),
            dma((REACH + 1,)),
            dma((4,)),
            dma((4,)),
        ],
        compiler_params=pltpu.CompilerParams(
            collective_id=0, has_side_effects=True, vmem_limit_bytes=40 << 20
        ),
        name="attention_backward",
    )(*(pltpu.with_memory_space_constraint(x, pltpu.HBM) for x in (queries, keys, values, outputs, out_grads, log_sums, doc_lengths)))
    shapes = [(TOK, HEADS * DIM), (TOK, DIM), (TOK, DIM)]
    return pl.pallas_call(
        functools.partial(finish, outer, inner),
        out_shape=[jax.ShapeDtypeStruct(shape, BF16) for shape in shapes],
        in_specs=[pl.BlockSpec(memory_space=pltpu.VMEM)] * 3,
        out_specs=[anywhere] * 3,
        scratch_shapes=[pltpu.VMEM((TOK, DIM), BF16), pltpu.VMEM((TOK, DIM), BF16), dma((3,))],
        compiler_params=pltpu.CompilerParams(vmem_limit_bytes=16 << 20),
        name="finish",
    )(*grads)


def solution(mesh):
    rows = P(("dp", "outer", "inner"), None)
    return jax.shard_map(
        functools.partial(local, mesh.shape["outer"], mesh.shape["inner"]),
        mesh=mesh,
        in_specs=(rows,) * 5 + (P(None, ("dp", "outer", "inner")), P("dp")),
        out_specs=(rows,) * 3,
        check_vma=False,
    )
```

```python
import functools
import math

import jax
import jax.numpy as jnp
from jax import lax
from jax.experimental import pallas as pl
from jax.experimental.pallas import tpu as pltpu
from jax.sharding import PartitionSpec as P

MESH = pl.DeviceIdType.MESH
F32 = jnp.float32
BF16 = jnp.bfloat16
HEADS = 8
DIM = 128
TOK = 256
GROUP = 2
REACH = 4


def nn(a, b):
    return lax.dot_general(a, b, (((1,), (0,)), ((), ())), preferred_element_type=F32)


def nt(a, b):
    return lax.dot_general(a, b, (((1,), (1,)), ((), ())), preferred_element_type=F32)


def kernel(
    outer, inner, q_hbm, k_hbm, v_hbm, o_hbm, g_hbm, lse_hbm, docs_hbm, dq_fin, own, ret_in,
    docs, qs, gs, qt, gt, os, rows, cols, kv, bias, start, probs, ds, ret_out, dq_out, dq_in,
    load_sem, kv_send, kv_recv, ret_send, ret_recv, sib_send, sib_recv,
):
    dp = lax.axis_index("dp")
    here = lax.axis_index("outer") * inner + lax.axis_index("inner")
    core = lax.rem(here, 2)
    y = lax.rem(here // 2, REACH)
    total = outer * inner
    scale = 1.0 / DIM**0.5
    log2e = math.log2(math.e)

    def device(index):
        index = lax.rem(index + total, total)
        return (dp, index // inner, lax.rem(index, inner))

    sibling = device(here + 1 - 2 * core)

    def ahead(k):
        return here + 2 * k < total

    def behind(k):
        return here - 2 * k >= 0

    barrier = pltpu.get_barrier_semaphore()
    pl.semaphore_signal(barrier, inc=1, device_id=sibling, device_id_type=MESH)
    for k in range(1, REACH + 1):
        for reaches, way in ((ahead, 1), (behind, -1)):

            @pl.when(reaches(k))
            def _():
                pl.semaphore_signal(
                    barrier, inc=1, device_id=device(here + way * 2 * k), device_id_type=MESH
                )

    loads = []

    def load(src, dst, n):
        copy = pltpu.make_async_copy(src, dst, load_sem.at[n])
        copy.start()
        loads.append(copy)

    load(k_hbm, kv.at[0, pl.ds(0, TOK)], 0)
    load(v_hbm, kv.at[0, pl.ds(TOK, TOK)], 1)
    for h in range(HEADS):
        load(q_hbm.at[:, pl.ds(h * DIM, DIM)], qs.at[0, pl.ds(h * TOK, TOK)], 2 + h)
        load(g_hbm.at[:, pl.ds(h * DIM, DIM)], gs.at[0, pl.ds(h * TOK, TOK)], 10 + h)
        load(o_hbm.at[:, pl.ds(h * DIM, DIM)], os.at[pl.ds(h * TOK, TOK)], 18 + h)
    load(lse_hbm, rows.at[0, pl.ds(0, HEADS)], 26)
    load(docs_hbm, docs, 27)

    greeted = jnp.int32(1)
    for k in range(1, REACH + 1):
        for reaches in (ahead, behind):
            greeted = greeted + jnp.where(reaches(k), 1, 0)
    pl.semaphore_wait(barrier, greeted)
    for copy in loads[:2]:
        copy.wait()

    def kv_copy(k):
        return pltpu.make_async_remote_copy(
            src_ref=kv.at[0], dst_ref=kv.at[k], send_sem=kv_send.at[k], recv_sem=kv_recv.at[k],
            device_id=device(here + 2 * k), device_id_type=MESH,
        )

    def ret_copy(k):
        return pltpu.make_async_remote_copy(
            src_ref=ret_out.at[k], dst_ref=ret_in.at[k], send_sem=ret_send.at[k], recv_sem=ret_recv.at[k],
            device_id=device(here - 2 * k), device_id_type=MESH,
        )

    def sib_copy(src, dst, n):
        return pltpu.make_async_remote_copy(
            src_ref=src, dst_ref=dst, send_sem=sib_send.at[n], recv_sem=sib_recv.at[n],
            device_id=sibling, device_id_type=MESH,
        )

    def send(slot):
        def start(k):
            kv_copy(k).start()

        pl.when((slot <= y) & ahead(REACH - y + slot))(lambda: start(REACH - y + slot))
        pl.when(slot + y <= REACH - 2)(lambda: start(slot + 1))

    for z_ in range(4):
        send(z_)
    for copy in loads[2:]:
        copy.wait()
    to_sib = [sib_copy(qs.at[0], qs.at[1], 0), sib_copy(gs.at[0], gs.at[1], 1)]
    for copy in to_sib:
        copy.start()

    line = lax.broadcasted_iota(jnp.int32, (TOK, DIM), 0)
    first = here * TOK
    other = (here + 1 - 2 * core) * TOK
    end = jnp.int32(0)
    low = [jnp.zeros((TOK, DIM), jnp.int32) for _ in range(2)]
    for d in range(docs.shape[0]):
        end = end + docs[d]
        low = [jnp.where(line + base >= end, end, x) for base, x in zip((first, other), low)]
    start[0] = low[0]
    start[1] = low[1]

    row = lax.broadcasted_iota(jnp.int32, (HEADS, DIM), 0)
    delta = jnp.zeros((HEADS, TOK), F32)
    for h in range(HEADS):
        part = pl.ds(h * TOK, TOK)
        prod = gs[0, part, :].astype(F32) * os[part, :].astype(F32)
        hi = prod.astype(BF16)
        lo = (prod - hi.astype(F32)).astype(BF16)
        pick = jnp.where(row == h, 1.0, 0.0).astype(BF16)
        delta = delta + (nt(pick, hi) + nt(pick, lo))
    rows[0, HEADS:, :] = delta
    rows[0, :HEADS, :] = rows[0, :HEADS, :] * log2e
    to_sib.append(sib_copy(rows.at[0], rows.at[1], 2))
    to_sib[2].start()

    def prepare(a):
        left = rows[a]
        terms = []
        for _ in range(3):
            terms.append(left.astype(BF16))
            left = left - terms[-1].astype(F32)
        columns = jnp.concatenate(terms, axis=0).T
        place = lax.broadcasted_iota(jnp.int32, (6 * HEADS, DIM), 0)
        for n in range(2 * HEADS):
            pick = jnp.where(lax.rem(place, 2 * HEADS) == n, 1.0, 0.0).astype(BF16)
            cols[a, n] = nn(columns, pick)
        for h in range(HEADS):
            part = pl.ds(h * TOK, TOK)
            flat = pl.ds(a * HEADS * TOK + h * TOK, TOK)
            qt[:, flat] = qs[a, part, :].T
            gt[:, flat] = gs[a, part, :].T

    def twice(x):
        return jnp.concatenate([x, x], axis=1)

    def pairs(k):
        keys = kv[k, :TOK, :]
        values = kv[k, TOK:, :]
        t = (here - 2 * k) * TOK + lax.broadcasted_iota(jnp.int32, (TOK, TOK), 1)
        for a, query_base in enumerate((first, other)):
            p = query_base + lax.broadcasted_iota(jnp.int32, (TOK, TOK), 0)
            bias[a] = jnp.where((t >= twice(start[a])) & (t <= p), 0.0, -jnp.inf)
        for n in range(2 * HEADS // GROUP):
            a, h0 = n * GROUP // HEADS, n * GROUP % HEADS
            part = pl.ds(h0 * TOK, GROUP * TOK)
            scores = nt(qs[a, part, :], keys)
            dprob = nt(gs[a, part, :], values)
            for m in range(GROUP):
                h = h0 + m
                mine = slice(m * TOK, (m + 1) * TOK)
                out = pl.ds((a * HEADS + h) * TOK, TOK)
                prob = jnp.exp2(scores[mine] * (scale * log2e) - twice(cols[a, h]) + bias[a])
                dscore = prob * (dprob[mine] - twice(cols[a, HEADS + h]))
                probs[out, :] = prob.astype(BF16)
                ds[k, out, :] = dscore.astype(BF16)
        half = HEADS * TOK
        dk = nn(qt[:, :half], ds[k, :half, :]) + nn(qt[:, half:], ds[k, half:, :])
        dv = nn(gt[:, :half], probs[:half, :]) + nn(gt[:, half:], probs[half:, :])
        return dk * scale, dv

    orders = ((4, 3, 1, 2), (1, 4, 3, 2), (1, 4, 2, 3), (1, 3, 2, 4))

    prepare(0)

    for copy in to_sib:
        copy.wait_recv()
    prepare(1)

    def block(step, _):
        k = jnp.int32(0)
        for place, order in enumerate(orders):
            for m, back in enumerate(order):
                k = jnp.where((y == place) & (step == m + 1), back, k)

        @pl.when((k > 0) & behind(k))
        def _():
            kv_copy(k).wait_recv()

        @pl.when((k > 0) & ~behind(k))
        def _():
            kv[k] = jnp.zeros_like(kv[k])

        dk, dv = pairs(k)

        @pl.when(k == 0)
        def _():
            own[:DIM, :] = dk
            own[DIM:, :] = dv

        @pl.when((k > 0) & behind(k))
        def _():
            ret_out[k, :DIM, :] = dk.astype(BF16)
            ret_out[k, DIM:, :] = dv.astype(BF16)
            ret_copy(k).start()

        return 0

    lax.fori_loop(0, REACH + 1, block, 0)

    half = HEADS * TOK
    part = sum(nn(ds[core + m, half:, :], kv[core + m, :TOK, :]) for m in range(REACH))
    dq_out[...] = (part * scale).astype(BF16)
    dq_copy = sib_copy(dq_out, dq_in, 3)
    dq_copy.start()
    for copy in to_sib:
        copy.wait_send()
    part = sum(nn(ds[m, :half, :], kv[m, :TOK, :]) for m in range(REACH + 1)) * scale
    dq_copy.wait_recv()
    both = part + dq_in[...].astype(F32)
    for h in range(HEADS):
        dq_fin[:, h * DIM : (h + 1) * DIM] = both[h * TOK : (h + 1) * TOK].astype(BF16)
    dq_copy.wait_send()
    for k in range(1, REACH + 1):
        pl.when(ahead(k))(kv_copy(k).wait_send)
        pl.when(behind(k))(ret_copy(k).wait_send)
    for k in range(1, REACH + 1):
        pl.when(ahead(k))(ret_copy(k).wait_recv)


def finish(outer, inner, dq, own, ret, dq_out, dk_out, dv_out, dk, dv, sem):
    here = lax.axis_index("outer") * inner + lax.axis_index("inner")
    writes = [
        pltpu.make_async_copy(a, b, sem.at[n])
        for n, (a, b) in enumerate(((dq, dq_out), (dk, dk_out), (dv, dv_out)))
    ]
    writes[0].start()
    total = own[...]
    for k in range(1, REACH + 1):
        total = total + jnp.where(here + 2 * k < outer * inner, ret[k].astype(F32), 0.0)
    dk[...] = total[:DIM, :].T.astype(BF16)
    writes[1].start()
    dv[...] = total[DIM:, :].T.astype(BF16)
    writes[2].start()
    for write in writes:
        write.wait()


def local(outer, inner, queries, keys, values, outputs, out_grads, log_sums, doc_lengths):
    wide = HEADS * TOK
    anywhere = pl.BlockSpec(memory_space=pl.ANY)
    dma = pltpu.SemaphoreType.DMA
    grads = pl.pallas_call(
        functools.partial(kernel, outer, inner),
        out_shape=[
            jax.ShapeDtypeStruct((TOK, HEADS * DIM), BF16),
            jax.ShapeDtypeStruct((2 * DIM, TOK), F32),
            jax.ShapeDtypeStruct((REACH + 1, 2 * DIM, TOK), BF16),
        ],
        in_specs=[anywhere] * 7,
        out_specs=[pl.BlockSpec(memory_space=pltpu.VMEM)] * 3,
        scratch_shapes=[
            pltpu.SMEM(doc_lengths.shape, jnp.int32),
            pltpu.VMEM((2, wide, DIM), BF16),
            pltpu.VMEM((2, wide, DIM), BF16),
            pltpu.VMEM((DIM, 2 * wide), BF16),
            pltpu.VMEM((DIM, 2 * wide), BF16),
            pltpu.VMEM((wide, DIM), BF16),
            pltpu.VMEM((2, 2 * HEADS, TOK), F32),
            pltpu.VMEM((2, 2 * HEADS, TOK, DIM), F32),
            pltpu.VMEM((REACH + 1, 2 * TOK, DIM), BF16),
            pltpu.VMEM((2, TOK, TOK), F32),
            pltpu.VMEM((2, TOK, DIM), jnp.int32),
            pltpu.VMEM((2 * wide, TOK), BF16),
            pltpu.VMEM((REACH + 1, 2 * wide, TOK), BF16),
            pltpu.VMEM((REACH + 1, 2 * DIM, TOK), BF16),
            pltpu.VMEM((wide, DIM), BF16),
            pltpu.VMEM((wide, DIM), BF16),
            dma((28,)),
            dma((REACH + 1,)),
            dma((REACH + 1,)),
            dma((REACH + 1,)),
            dma((REACH + 1,)),
            dma((4,)),
            dma((4,)),
        ],
        compiler_params=pltpu.CompilerParams(
            collective_id=0, has_side_effects=True, vmem_limit_bytes=40 << 20
        ),
        name="attention_backward",
    )(*(pltpu.with_memory_space_constraint(x, pltpu.HBM) for x in (queries, keys, values, outputs, out_grads, log_sums, doc_lengths)))
    shapes = [(TOK, HEADS * DIM), (TOK, DIM), (TOK, DIM)]
    return pl.pallas_call(
        functools.partial(finish, outer, inner),
        out_shape=[jax.ShapeDtypeStruct(shape, BF16) for shape in shapes],
        in_specs=[pl.BlockSpec(memory_space=pltpu.VMEM)] * 3,
        out_specs=[anywhere] * 3,
        scratch_shapes=[pltpu.VMEM((TOK, DIM), BF16), pltpu.VMEM((TOK, DIM), BF16), dma((3,))],
        compiler_params=pltpu.CompilerParams(vmem_limit_bytes=16 << 20),
        name="finish",
    )(*grads)


def solution(mesh):
    rows = P(("dp", "outer", "inner"), None)
    return jax.shard_map(
        functools.partial(local, mesh.shape["outer"], mesh.shape["inner"]),
        mesh=mesh,
        in_specs=(rows,) * 5 + (P(None, ("dp", "outer", "inner")), P("dp")),
        out_specs=(rows,) * 3,
        check_vma=False,
    )
```

```python
import functools
import math

import jax
import jax.numpy as jnp
from jax import lax
from jax.experimental import pallas as pl
from jax.experimental.pallas import tpu as pltpu
from jax.sharding import PartitionSpec as P

MESH = pl.DeviceIdType.MESH
F32 = jnp.float32
BF16 = jnp.bfloat16
HEADS = 8
DIM = 128
TOK = 256
GROUP = 2
REACH = 4


def nn(a, b):
    return lax.dot_general(a, b, (((1,), (0,)), ((), ())), preferred_element_type=F32)


def nt(a, b):
    return lax.dot_general(a, b, (((1,), (1,)), ((), ())), preferred_element_type=F32)


def kernel(
    outer, inner, q_hbm, k_hbm, v_hbm, o_hbm, g_hbm, lse_hbm, docs_hbm, dq_fin, own, ret_in,
    docs, qs, gs, qt, gt, os, rows, cols, kv, bias, start, probs, ds, both, ret_out, dq_out, dq_in,
    load_sem, kv_send, kv_recv, ret_send, ret_recv, sib_send, sib_recv,
):
    dp = lax.axis_index("dp")
    here = lax.axis_index("outer") * inner + lax.axis_index("inner")
    core = lax.rem(here, 2)
    y = lax.rem(here // 2, REACH)
    total = outer * inner
    scale = 1.0 / DIM**0.5
    log2e = math.log2(math.e)

    def device(index):
        index = lax.rem(index + total, total)
        return (dp, index // inner, lax.rem(index, inner))

    sibling = device(here + 1 - 2 * core)

    def ahead(k):
        return here + 2 * k < total

    def behind(k):
        return here - 2 * k >= 0

    barrier = pltpu.get_barrier_semaphore()
    pl.semaphore_signal(barrier, inc=1, device_id=sibling, device_id_type=MESH)
    for k in range(1, REACH + 1):
        for reaches, way in ((ahead, 1), (behind, -1)):

            @pl.when(reaches(k))
            def _():
                pl.semaphore_signal(
                    barrier, inc=1, device_id=device(here + way * 2 * k), device_id_type=MESH
                )

    loads = []

    def load(src, dst, n):
        copy = pltpu.make_async_copy(src, dst, load_sem.at[n])
        copy.start()
        loads.append(copy)

    load(k_hbm, kv.at[0, pl.ds(0, TOK)], 0)
    load(v_hbm, kv.at[0, pl.ds(TOK, TOK)], 1)
    for h in range(HEADS):
        load(q_hbm.at[:, pl.ds(h * DIM, DIM)], qs.at[0, pl.ds(h * TOK, TOK)], 2 + h)
        load(g_hbm.at[:, pl.ds(h * DIM, DIM)], gs.at[0, pl.ds(h * TOK, TOK)], 10 + h)
        load(o_hbm.at[:, pl.ds(h * DIM, DIM)], os.at[pl.ds(h * TOK, TOK)], 18 + h)
    load(lse_hbm, rows.at[0, pl.ds(0, HEADS)], 26)
    load(docs_hbm, docs, 27)

    greeted = jnp.int32(1)
    for k in range(1, REACH + 1):
        for reaches in (ahead, behind):
            greeted = greeted + jnp.where(reaches(k), 1, 0)
    pl.semaphore_wait(barrier, greeted)
    for copy in loads[:2]:
        copy.wait()

    def kv_copy(k):
        return pltpu.make_async_remote_copy(
            src_ref=kv.at[0], dst_ref=kv.at[k], send_sem=kv_send.at[k], recv_sem=kv_recv.at[k],
            device_id=device(here + 2 * k), device_id_type=MESH,
        )

    def ret_copy(k):
        return pltpu.make_async_remote_copy(
            src_ref=ret_out.at[k], dst_ref=ret_in.at[k], send_sem=ret_send.at[k], recv_sem=ret_recv.at[k],
            device_id=device(here - 2 * k), device_id_type=MESH,
        )

    def sib_copy(src, dst, n):
        return pltpu.make_async_remote_copy(
            src_ref=src, dst_ref=dst, send_sem=sib_send.at[n], recv_sem=sib_recv.at[n],
            device_id=sibling, device_id_type=MESH,
        )

    def send(slot):
        def start(k):
            kv_copy(k).start()

        pl.when((slot <= y) & ahead(REACH - y + slot))(lambda: start(REACH - y + slot))
        pl.when(slot + y <= REACH - 2)(lambda: start(slot + 1))

    for z_ in range(4):
        send(z_)
    for copy in loads[2:]:
        copy.wait()
    to_sib = [sib_copy(qs.at[0], qs.at[1], 0), sib_copy(gs.at[0], gs.at[1], 1)]
    for copy in to_sib:
        copy.start()

    line = lax.broadcasted_iota(jnp.int32, (TOK, DIM), 0)
    first = here * TOK
    other = (here + 1 - 2 * core) * TOK
    end = jnp.int32(0)
    low = [jnp.zeros((TOK, DIM), jnp.int32) for _ in range(2)]
    for d in range(docs.shape[0]):
        end = end + docs[d]
        low = [jnp.where(line + base >= end, end, x) for base, x in zip((first, other), low)]
    start[0] = low[0]
    start[1] = low[1]

    row = lax.broadcasted_iota(jnp.int32, (HEADS, DIM), 0)
    delta = jnp.zeros((HEADS, TOK), F32)
    for h in range(HEADS):
        part = pl.ds(h * TOK, TOK)
        prod = gs[0, part, :].astype(F32) * os[part, :].astype(F32)
        hi = prod.astype(BF16)
        lo = (prod - hi.astype(F32)).astype(BF16)
        pick = jnp.where(row == h, 1.0, 0.0).astype(BF16)
        delta = delta + (nt(pick, hi) + nt(pick, lo))
    rows[0, HEADS:, :] = delta
    rows[0, :HEADS, :] = rows[0, :HEADS, :] * log2e
    to_sib.append(sib_copy(rows.at[0], rows.at[1], 2))
    to_sib[2].start()

    def prepare(a):
        left = rows[a]
        terms = []
        for _ in range(3):
            terms.append(left.astype(BF16))
            left = left - terms[-1].astype(F32)
        columns = jnp.concatenate(terms, axis=0).T
        place = lax.broadcasted_iota(jnp.int32, (6 * HEADS, DIM), 0)
        for n in range(2 * HEADS):
            pick = jnp.where(lax.rem(place, 2 * HEADS) == n, 1.0, 0.0).astype(BF16)
            cols[a, n] = nn(columns, pick)
        for h in range(HEADS):
            part = pl.ds(h * TOK, TOK)
            flat = pl.ds(a * HEADS * TOK + h * TOK, TOK)
            qt[:, flat] = qs[a, part, :].T
            gt[:, flat] = gs[a, part, :].T

    def twice(x):
        return jnp.concatenate([x, x], axis=1)

    def pairs(k, sides):
        keys = kv[k, :TOK, :]
        values = kv[k, TOK:, :]
        t = (here - 2 * k) * TOK + lax.broadcasted_iota(jnp.int32, (TOK, TOK), 1)
        for a, query_base in enumerate((first, other)[:sides]):
            p = query_base + lax.broadcasted_iota(jnp.int32, (TOK, TOK), 0)
            bias[a] = jnp.where((t >= twice(start[a])) & (t <= p), 0.0, -jnp.inf)
        for n in range(sides * HEADS // GROUP):
            a, h0 = n * GROUP // HEADS, n * GROUP % HEADS
            part = pl.ds(h0 * TOK, GROUP * TOK)
            scores = nt(qs[a, part, :], keys)
            dprob = nt(gs[a, part, :], values)
            for m in range(GROUP):
                h = h0 + m
                mine = slice(m * TOK, (m + 1) * TOK)
                out = pl.ds((a * HEADS + h) * TOK, TOK)
                prob = jnp.exp2(scores[mine] * (scale * log2e) - twice(cols[a, h]) + bias[a])
                dscore = prob * (dprob[mine] - twice(cols[a, HEADS + h]))
                probs[out, :] = prob.astype(BF16)
                ds[k, out, :] = dscore.astype(BF16)
        half = HEADS * TOK
        dk = nn(qt[:, :half], ds[k, :half, :])
        dv = nn(gt[:, :half], probs[:half, :])
        if sides == 2:
            dk = dk + nn(qt[:, half:], ds[k, half:, :])
            dv = dv + nn(gt[:, half:], probs[half:, :])
        both[:DIM, :] = dk * scale
        both[DIM:, :] = dv

    orders = ((4, 3, 1, 2), (1, 4, 3, 2), (1, 4, 2, 3), (1, 3, 2, 4))

    prepare(0)

    for copy in to_sib:
        copy.wait_recv()
    prepare(1)

    def block(step, _):
        k = jnp.int32(0)
        for place, order in enumerate(orders):
            for m, back in enumerate(order):
                k = jnp.where((y == place) & (step == m + 1), back, k)

        @pl.when((k > 0) & behind(k))
        def _():
            kv_copy(k).wait_recv()

        @pl.when((k > 0) & ~behind(k))
        def _():
            kv[k] = jnp.zeros_like(kv[k])

        near = (k >= core) & (k < core + REACH)
        pl.when(near)(lambda: pairs(k, 2))
        pl.when(~near)(lambda: pairs(k, 1))

        @pl.when(k == 0)
        def _():
            own[...] = both[...]

        @pl.when((k > 0) & behind(k))
        def _():
            ret_out[k] = both[...].astype(BF16)
            ret_copy(k).start()

        return 0

    lax.fori_loop(0, REACH + 1, block, 0)

    half = HEADS * TOK
    part = sum(nn(ds[core + m, half:, :], kv[core + m, :TOK, :]) for m in range(REACH))
    dq_out[...] = (part * scale).astype(BF16)
    dq_copy = sib_copy(dq_out, dq_in, 3)
    dq_copy.start()
    for copy in to_sib:
        copy.wait_send()
    part = sum(nn(ds[m, :half, :], kv[m, :TOK, :]) for m in range(REACH + 1)) * scale
    dq_copy.wait_recv()
    query = part + dq_in[...].astype(F32)
    for h in range(HEADS):
        dq_fin[:, h * DIM : (h + 1) * DIM] = query[h * TOK : (h + 1) * TOK].astype(BF16)
    dq_copy.wait_send()
    for k in range(1, REACH + 1):
        pl.when(ahead(k))(kv_copy(k).wait_send)
        pl.when(behind(k))(ret_copy(k).wait_send)
    for k in range(1, REACH + 1):
        pl.when(ahead(k))(ret_copy(k).wait_recv)


def finish(outer, inner, dq, own, ret, dq_out, dk_out, dv_out, dk, dv, sem):
    here = lax.axis_index("outer") * inner + lax.axis_index("inner")
    writes = [
        pltpu.make_async_copy(a, b, sem.at[n])
        for n, (a, b) in enumerate(((dq, dq_out), (dk, dk_out), (dv, dv_out)))
    ]
    writes[0].start()
    total = own[...]
    for k in range(1, REACH + 1):
        total = total + jnp.where(here + 2 * k < outer * inner, ret[k].astype(F32), 0.0)
    dk[...] = total[:DIM, :].T.astype(BF16)
    writes[1].start()
    dv[...] = total[DIM:, :].T.astype(BF16)
    writes[2].start()
    for write in writes:
        write.wait()


def local(outer, inner, queries, keys, values, outputs, out_grads, log_sums, doc_lengths):
    wide = HEADS * TOK
    anywhere = pl.BlockSpec(memory_space=pl.ANY)
    dma = pltpu.SemaphoreType.DMA
    grads = pl.pallas_call(
        functools.partial(kernel, outer, inner),
        out_shape=[
            jax.ShapeDtypeStruct((TOK, HEADS * DIM), BF16),
            jax.ShapeDtypeStruct((2 * DIM, TOK), F32),
            jax.ShapeDtypeStruct((REACH + 1, 2 * DIM, TOK), BF16),
        ],
        in_specs=[anywhere] * 7,
        out_specs=[pl.BlockSpec(memory_space=pltpu.VMEM)] * 3,
        scratch_shapes=[
            pltpu.SMEM(doc_lengths.shape, jnp.int32),
            pltpu.VMEM((2, wide, DIM), BF16),
            pltpu.VMEM((2, wide, DIM), BF16),
            pltpu.VMEM((DIM, 2 * wide), BF16),
            pltpu.VMEM((DIM, 2 * wide), BF16),
            pltpu.VMEM((wide, DIM), BF16),
            pltpu.VMEM((2, 2 * HEADS, TOK), F32),
            pltpu.VMEM((2, 2 * HEADS, TOK, DIM), F32),
            pltpu.VMEM((REACH + 1, 2 * TOK, DIM), BF16),
            pltpu.VMEM((2, TOK, TOK), F32),
            pltpu.VMEM((2, TOK, DIM), jnp.int32),
            pltpu.VMEM((2 * wide, TOK), BF16),
            pltpu.VMEM((REACH + 1, 2 * wide, TOK), BF16),
            pltpu.VMEM((2 * DIM, TOK), F32),
            pltpu.VMEM((REACH + 1, 2 * DIM, TOK), BF16),
            pltpu.VMEM((wide, DIM), BF16),
            pltpu.VMEM((wide, DIM), BF16),
            dma((28,)),
            dma((REACH + 1,)),
            dma((REACH + 1,)),
            dma((REACH + 1,)),
            dma((REACH + 1,)),
            dma((4,)),
            dma((4,)),
        ],
        compiler_params=pltpu.CompilerParams(
            collective_id=0, has_side_effects=True, vmem_limit_bytes=40 << 20
        ),
        name="attention_backward",
    )(*(pltpu.with_memory_space_constraint(x, pltpu.HBM) for x in (queries, keys, values, outputs, out_grads, log_sums, doc_lengths)))
    shapes = [(TOK, HEADS * DIM), (TOK, DIM), (TOK, DIM)]
    return pl.pallas_call(
        functools.partial(finish, outer, inner),
        out_shape=[jax.ShapeDtypeStruct(shape, BF16) for shape in shapes],
        in_specs=[pl.BlockSpec(memory_space=pltpu.VMEM)] * 3,
        out_specs=[anywhere] * 3,
        scratch_shapes=[pltpu.VMEM((TOK, DIM), BF16), pltpu.VMEM((TOK, DIM), BF16), dma((3,))],
        compiler_params=pltpu.CompilerParams(vmem_limit_bytes=16 << 20),
        name="finish",
    )(*grads)


def solution(mesh):
    rows = P(("dp", "outer", "inner"), None)
    return jax.shard_map(
        functools.partial(local, mesh.shape["outer"], mesh.shape["inner"]),
        mesh=mesh,
        in_specs=(rows,) * 5 + (P(None, ("dp", "outer", "inner")), P("dp")),
        out_specs=(rows,) * 3,
        check_vma=False,
    )
```
